32 devices in a mesh: grp: 2 (over y), clu: 4 (over z), row: 4 (over x, core).
Axes of the slice: x: 2, y: 2, z: 4, core: 2. Of those that a mesh axis runs over, the one named last changes fastest.
Arguments:
- slip: float32 [8192, 256], P(('grp', 'clu', 'row')), parts along dimension 0, may hold values from -6 to 6
- state: float32 [8192, 256], P(('grp', 'clu', 'row')), parts along dimension 0, may hold values from 0 to 1
- load: float32 [8192, 256], P(('grp', 'clu', 'row')), parts along dimension 0, may hold values from -6 to 6
- friction_a: float32 [8192], P(('grp', 'clu', 'row')), parts along dimension 0, may hold values from 1 to 3
- near_blocks: bfloat16 [3584, 128, 128], P(('grp', 'clu', 'row')), parts along dimension 0, may hold values from -0.0625 to 0.0625
- near_pairs: int32 [3584, 2], P(('grp', 'clu', 'row')), parts along dimension 0, may hold values from 0 to 31, as said below
- far_u: bfloat16 [128, 4, 32, 256], P(('grp', 'clu', 'row')), parts along dimension 0, may hold values from -0.25 to 0.25
- far_v: bfloat16 [128, 4, 32, 256], P(('grp', 'clu', 'row')), parts along dimension 0, may hold values from -0.375 to 0.375
- far_rank: int32 [128, 4], P(('grp', 'clu', 'row')), parts along dimension 0, may hold values from 1 to 32
Outputs:
- slip_next: float32 [8192, 256], P(('grp', 'clu', 'row')), parts along dimension 0
- state_next: float32 [8192, 256], P(('grp', 'clu', 'row')), parts along dimension 0
The draws below stay inside these ranges and needn't reach their ends.
There are 2 independent parts, one for each index of `grp`. The reference program is written for one: setup_inputs(seed, part) draws one part's arguments, and reference() takes and returns one part's arrays. A program takes and returns all parts, laid end to end along the dimension named above; each array names one. Nothing has to cross between parts.
Inputs may be any that keep to these rules, and one draw needn't show every extreme that they name: `near_pairs`: rows k * 112 to (k + 1) * 112 - 1 belong to device k = c * 4 + r of clu+row; their target cluster lies in group c (clusters c * 8 to (c + 1) * 8 - 1) and their source cluster within 4 clusters of the target. Pairs may repeat; their blocks add.
All inputs are finite; a program needn't handle non-finite values.
Results may differ from the reference program's by a relative error of at most 0.00036.
Values may be sent and summed in bfloat16 or wider, within the bound.
No kernel may reach another device: no remote copies, remote signals or barrier semaphores. Data moves between devices by JAX's collectives and lax.ppermute only.
A program may use at most 128 MiB of HBM per device.

```python
import math
import jax
import jax.numpy as jnp
from jax import lax

B = 128
R = 32
M = 256
C_DEV = 2
NEAR_DEV = 112
REACH = 4
CPD = 8
NC = 32
E_DEV = 256
ELEMS = 4096
NEAR = 1792
FARS = 64
N_CLU = 4
N_ROW = 4


def draw_near_pairs(key, part):
    key = jax.random.fold_in(key, 11)
    first_key, second_key = jax.random.split(key)
    slots = jnp.arange(NEAR, dtype=jnp.int32)
    group = slots // (NEAR_DEV * (CPD // C_DEV))
    target = group * CPD + jax.random.randint(first_key, (NEAR,), 0, CPD, dtype=jnp.int32)
    offset = jax.random.randint(second_key, (NEAR,), -REACH, REACH + 1, dtype=jnp.int32)
    within = slots % NEAR_DEV
    offset = jnp.where(within == 0, -REACH, jnp.where(within == 1, REACH, offset))
    source = jnp.clip(target + offset, 0, NC - 1)
    return jnp.stack([target, source], axis=1).astype(jnp.int32)


def touch_ends(array, own_key, low, largest):
    dims = array.shape
    place = [jax.random.randint(jax.random.fold_in(own_key, axis), (), 0, dims[axis]) for axis in range(len(dims))]
    array = array.at[tuple(place)].set(low)
    longest = dims.index(max(dims))
    place[longest] = (place[longest] + 1) % dims[longest]
    return array.at[tuple(place)].set(largest)


def level_of(key, extent, cuts, low, high):
    def one(axis_at, parts):
        steps = jax.random.uniform(jax.random.fold_in(jax.random.fold_in(key, 6), axis_at), (parts,), jnp.float32, low / len(cuts), high / len(cuts))
        return jnp.repeat(jnp.exp(steps), extent[axis_at] // parts).reshape((-1,) + (1,) * (len(extent) - axis_at - 1))

    gain = one(*cuts[0])
    for cut in cuts[1:]:
        gain = gain * one(*cut)
    return gain


def scatter_about(stream_key, extent, deviation, bound, shards=(), kind=jnp.bfloat16):
    values = jax.random.normal(stream_key, extent, jnp.float32) * deviation
    if len(shards) > 0:
        values = level_of(stream_key, extent, shards, -0.22, 0.18) * values
    return jnp.clip(values, min=-bound, max=bound).astype(kind)


def setup_inputs(seed: int = 0, part: int = 0) -> dict:
    keys = jax.random.split(jax.random.key(seed), 10)
    own_keys = jax.random.split(jax.random.fold_in(keys[9], part), 10)
    return {
        "slip": scatter_about(own_keys[0], (ELEMS, M), 1.0, 6.0, ((0, 16),), jnp.float32),
        "state": jnp.clip(1.0 * jax.random.uniform(own_keys[1], (ELEMS, M), jnp.float32) ** level_of(own_keys[1], (ELEMS, M), ((0, 16),), -0.2, 0.2), 0.0, 1.0),
        "load": scatter_about(own_keys[2], (ELEMS, M), 1.0, 6.0, ((0, 16),), jnp.float32),
        "friction_a": jnp.clip(jnp.exp(math.log(3.0) - 1.0986123 * jax.random.uniform(own_keys[3], (ELEMS,), jnp.float32) ** level_of(own_keys[3], (ELEMS,), ((0, 16),), -0.2, 0.2)), 1.0, 3.0),
        "near_blocks": scatter_about(own_keys[4], (NEAR, B, B), (B * NEAR_DEV // C_DEV) ** -0.5, 0.0625, ((0, 16),)),
        "near_pairs": draw_near_pairs(jax.random.fold_in(jax.random.fold_in(keys[9], part), 71), part),
        "far_u": scatter_about(own_keys[6], (FARS, N_CLU, R, E_DEV), (R * N_CLU * N_ROW) ** -0.5, 0.25, ((0, 16),)),
        "far_v": scatter_about(own_keys[7], (FARS, N_CLU, R, E_DEV), E_DEV ** -0.5, 0.375, ((0, 16),)),
        "far_rank": touch_ends(jax.random.randint(own_keys[8], (FARS, N_CLU), 1, R + 1), jax.random.fold_in(own_keys[8], 1), 1, R).astype(jnp.int32),
    }


step_size = 0.2


def slip_rates(stress, state, load, friction_a):
    softness = friction_a[:, None]
    velocity = 2.0 * jnp.exp(-state / softness) * jnp.sinh((stress + load) / (2.0 * softness))
    speed = jnp.abs(velocity)
    drift = jnp.exp(-state) - speed / (1.0 + speed)
    return velocity, drift


def reference(slip, state, load, friction_a, near_blocks, near_pairs, far_u, far_v, far_rank):
    devices = N_CLU * N_ROW

    def stress_of(field):
        half = lax.optimization_barrier(field.astype(jnp.bfloat16))
        tiles = half.reshape(NC, B, M)
        blocks = near_blocks.reshape(devices, NEAR_DEV, B, B)
        pairs = near_pairs.reshape(devices, NEAR_DEV, 2)

        def near_step(total, item):
            block_set, pair_set = item
            picked = jnp.take(tiles, pair_set[:, 1], axis=0).astype(jnp.float32)
            product = jnp.einsum("kij,kjm->kim", block_set.astype(jnp.float32), picked,
                                 precision=lax.Precision.HIGHEST)
            return total.at[pair_set[:, 0]].add(product), None

        near_total, _ = lax.scan(near_step, jnp.zeros((NC, B, M), jnp.float32), (blocks, pairs))
        owned = half.reshape(N_CLU, N_ROW, E_DEV, M)
        basis_out = far_u.reshape(devices, N_ROW, N_CLU, R, E_DEV)
        basis_in = far_v.reshape(devices, N_ROW, N_CLU, R, E_DEV)
        ranks = far_rank.reshape(devices, N_ROW, N_CLU)

        def far_step(total, item):
            holder, out_set, in_set, rank_set = item
            group = holder // N_ROW
            column = holder % N_ROW
            sources = jnp.take(owned, column, axis=1).astype(jnp.float32)
            coeffs = jnp.einsum("tkre,kem->tkrm", in_set.astype(jnp.float32), sources,
                                precision=lax.Precision.HIGHEST)
            index = lax.broadcasted_iota(jnp.int32, (1, 1, R, 1), 2)
            coeffs = jnp.where(index < rank_set[:, :, None, None], coeffs, 0.0)
            coeffs = lax.optimization_barrier(coeffs.astype(jnp.bfloat16)).astype(jnp.float32)
            contrib = jnp.einsum("tkre,tkrm->tem", out_set.astype(jnp.float32), coeffs,
                                 precision=lax.Precision.HIGHEST)
            return total.at[group].add(contrib), None

        holders = jnp.arange(devices, dtype=jnp.int32)
        far_total, _ = lax.scan(far_step, jnp.zeros((N_CLU, N_ROW, E_DEV, M), jnp.float32),
                                (holders, basis_out, basis_in, ranks))
        return near_total.reshape(ELEMS, M) + far_total.reshape(ELEMS, M)

    velocity_one, drift_one = slip_rates(stress_of(slip), state, load, friction_a)
    slip_mid = slip + step_size * velocity_one
    state_mid = state + step_size * drift_one
    velocity_two, drift_two = slip_rates(stress_of(slip_mid), state_mid, load, friction_a)
    slip_next = slip + 0.5 * step_size * (velocity_one + velocity_two)
    state_next = state + 0.5 * step_size * (drift_one + drift_two)
    return (slip_next, state_next)
```

```python
import functools

import jax
import jax.numpy as jnp
from jax import lax
from jax.experimental import pallas as pl
from jax.experimental.pallas import tpu as pltpu
from jax.sharding import PartitionSpec as P

REACH = 4
CORES = 2
STEP = 0.2
UNROLL = 16


def core_swap(array):
    devices = lax.axis_size("row")
    return lax.ppermute(array, "row", [(i, i ^ 1) for i in range(devices)])


def chip_shift(array, step):
    devices = lax.axis_size("row")
    pairs = [(i, (i + CORES * step) % devices) for i in range(devices)]
    return lax.ppermute(array, "row", pairs)


def group_shift(array, step):
    groups = lax.axis_size("clu")
    return lax.ppermute(array, "clu", [(i, (i + step) % groups) for i in range(groups)])


def group_next(array, step):
    groups = lax.axis_size("clu")
    pairs = [(i, i + step) for i in range(groups) if 0 <= i + step < groups]
    return lax.ppermute(array, "clu", pairs)


def stress_kernel(leaf, src, dst, place, blocks, window, far_u, coeffs, out):
    targets, groups, rank, elems = far_u.shape
    members = window.shape[1]
    chips = targets // CORES
    group, chip, core = place[0], place[1], place[2]
    for other in range(CORES):
        for ahead in range(chips):
            target = lax.rem(chip + ahead, chips) * CORES + (core ^ other)
            bases = [far_u[target, lax.rem(group + s, groups)] for s in range(groups)]
            parts = [coeffs[s, target] for s in range(groups)]
            out[pl.ds((other * chips + ahead) * elems, elems), :] = lax.dot_general(
                jnp.concatenate(bases, axis=0),
                jnp.concatenate(parts, axis=0),
                (((0,), (0,)), ((), ())),
                preferred_element_type=jnp.float32,
            )
    count = blocks.shape[0]
    unroll = UNROLL if count % UNROLL == 0 else 1

    def step(i, carry):
        products = []
        for u in range(unroll):
            j = i * unroll + u
            rows = window[pl.ds(pl.multiple_of(src[j] * leaf, leaf), leaf), :]
            products.append(jnp.dot(blocks[j], rows, preferred_element_type=jnp.float32))
        for u in range(unroll):
            j = i * unroll + u
            out[pl.ds(pl.multiple_of(dst[j] * leaf, leaf), leaf), :] += products[u]
        return carry

    lax.fori_loop(0, count // unroll, step, 0)


def partial_stress(src, dst, place, blocks, window, far_u, coeffs):
    targets, groups, rank, elems = far_u.shape
    count, leaf, _ = blocks.shape
    members = window.shape[1]
    vmem = pl.BlockSpec(memory_space=pltpu.VMEM)
    smem = pl.BlockSpec(memory_space=pltpu.SMEM)
    return pl.pallas_call(
        functools.partial(stress_kernel, leaf),
        out_shape=jax.ShapeDtypeStruct((targets * elems, members), jnp.float32),
        in_specs=[smem, smem, smem, vmem, vmem, vmem, vmem],
        out_specs=vmem,
        compiler_params=pltpu.CompilerParams(vmem_limit_bytes=40 * 1024 * 1024),
        cost_estimate=pl.CostEstimate(
            flops=2 * members * (count * leaf * leaf + targets * groups * rank * elems),
            bytes_accessed=2 * count * leaf * leaf + 8 * targets * elems * members,
            transcendentals=0,
        ),
    )(src, dst, place, blocks, window, far_u, coeffs)


def slip_rates(stress, state, load, friction_a):
    softness = friction_a[:, None]
    velocity = 2.0 * jnp.exp(-state / softness) * jnp.sinh((stress + load) / (2.0 * softness))
    speed = jnp.abs(velocity)
    drift = jnp.exp(-state) - speed / (1.0 + speed)
    return (velocity, drift)


def body(slip, state, load, friction_a, near_blocks, near_pairs, far_u, far_v, far_rank):
    elems, members = slip.shape
    leaf = near_blocks.shape[1]
    own = elems // leaf
    devices, groups = lax.axis_size("row"), lax.axis_size("clu")
    chips = devices // CORES
    clusters = devices * own
    assert REACH <= CORES * own
    group, row = lax.axis_index("clu"), lax.axis_index("row")
    chip, core = row // CORES, row % CORES
    place = jnp.stack([group, chip, core]).astype(jnp.int32)

    source = near_pairs[:, 1] - group * clusters
    before, after = source < 0, source >= clusters
    local = jnp.where(before, source + clusters, jnp.where(after, source - clusters, source))
    holder = local // own
    piece = jnp.where(
        before,
        chips,
        jnp.where(after, chips + 1, (chip - holder // CORES + chips) % chips),
    )
    other = (holder % CORES) ^ core
    src = ((other * (chips + 2) + piece) * own + local % own).astype(jnp.int32)
    target = near_pairs[:, 0] - group * clusters
    owner = target // own
    ahead = (owner // CORES - chip + chips) % chips
    dst = ((((owner % CORES) ^ core) * chips + ahead) * own + target % own).astype(jnp.int32)

    rank = far_u.shape[2]
    column = lax.broadcasted_iota(jnp.int32, (1, 1, rank, 1), 2)
    bases = jnp.where(column < far_rank[:, :, None, None], far_v, jnp.zeros_like(far_v))
    held = []
    for s in range(groups):
        there = lax.dynamic_index_in_dim(bases, (group + s) % groups, axis=1, keepdims=False)
        held.append(there if s == 0 else group_shift(there, s))
    held = jnp.stack(held).reshape(groups * devices * rank, elems)

    def section_stress(field):
        half = field.astype(jnp.bfloat16)
        coeffs = jnp.dot(held, half, preferred_element_type=jnp.float32).astype(jnp.bfloat16)
        coeffs = coeffs.reshape(groups, devices, rank, members)
        coeffs = jnp.stack(
            [coeffs[s] if s == 0 else group_shift(coeffs[s], -s) for s in range(groups)]
        )
        pieces = [half] + [chip_shift(half, s) for s in range(1, chips)]
        near = jnp.stack(pieces)
        last = lax.dynamic_index_in_dim(near, (chip + 1) % chips, axis=0, keepdims=False)
        first = lax.dynamic_index_in_dim(near, chip, axis=0, keepdims=False)
        ends = jnp.stack([group_next(last, 1), group_next(first, -1)])
        window = jnp.concatenate([near, ends, core_swap(near), core_swap(ends)], axis=0)
        window = window.reshape(-1, members)
        partial = partial_stress(src, dst, place, near_blocks, window, far_u, coeffs)
        partial = partial.reshape(CORES, chips, elems, members)
        joined = [partial[0, s] + core_swap(partial[1, s]) for s in range(chips)]
        total = joined[0]
        for s in range(1, chips):
            total = total + chip_shift(joined[s].astype(jnp.bfloat16), s).astype(jnp.float32)
        return total

    velocity_one, drift_one = slip_rates(section_stress(slip), state, load, friction_a)
    slip_mid = slip + STEP * velocity_one
    state_mid = state + STEP * drift_one
    velocity_two, drift_two = slip_rates(section_stress(slip_mid), state_mid, load, friction_a)
    slip_next = slip + 0.5 * STEP * (velocity_one + velocity_two)
    state_next = state + 0.5 * STEP * (drift_one + drift_two)
    return (slip_next, state_next)


def solution(mesh):
    placed = (
        P(("grp", "clu", "row"), None),
        P(("grp", "clu", "row"), None),
        P(("grp", "clu", "row"), None),
        P(("grp", "clu", "row")),
        P(("grp", "clu", "row"), None, None),
        P(("grp", "clu", "row"), None),
        P(("grp", "clu", "row"), None, None, None),
        P(("grp", "clu", "row"), None, None, None),
        P(("grp", "clu", "row"), None),
    )
    return jax.shard_map(
        body,
        mesh=mesh,
        in_specs=placed,
        out_specs=(P(("grp", "clu", "row"), None), P(("grp", "clu", "row"), None)),
        check_vma=False,
    )
```

```python
import functools

import jax
import jax.numpy as jnp
from jax import lax
from jax.experimental import pallas as pl
from jax.experimental.pallas import tpu as pltpu
from jax.sharding import PartitionSpec as P

REACH = 4
CORES = 2
STEP = 0.2
UNROLL = 16


def core_swap(array):
    devices = lax.axis_size("row")
    return lax.ppermute(array, "row", [(i, i ^ 1) for i in range(devices)])


def chip_shift(array, step):
    devices = lax.axis_size("row")
    pairs = [(i, (i + CORES * step) % devices) for i in range(devices)]
    return lax.ppermute(array, "row", pairs)


def group_shift(array, step):
    groups = lax.axis_size("clu")
    return lax.ppermute(array, "clu", [(i, (i + step) % groups) for i in range(groups)])


def gathered_blocks(leaf, inside, src, dst, blocks, window, out, block_list, row_list):
    count = blocks.shape[0]
    spare = out.shape[0] // leaf - 1

    def sort(j, found):
        block_list[found] = j
        row_list[found] = dst[j]
        return found + inside(src[j]).astype(jnp.int32)

    found = lax.fori_loop(0, count, sort, jnp.int32(0), unroll=8)
    for u in range(UNROLL):
        block_list[found + u] = 0
        row_list[found + u] = spare

    def step(i, carry):
        products = []
        for u in range(UNROLL):
            j = block_list[i * UNROLL + u]
            row = lax.rem(src[j], window.shape[0] // leaf)
            rows = window[pl.ds(pl.multiple_of(row * leaf, leaf), leaf), :]
            products.append(jnp.dot(blocks[j], rows, preferred_element_type=jnp.float32))
        for u in range(UNROLL):
            row = row_list[i * UNROLL + u]
            out[pl.ds(pl.multiple_of(row * leaf, leaf), leaf), :] += products[u]
        return carry

    lax.fori_loop(0, pl.cdiv(found, UNROLL), step, 0)


def inner_kernel(leaf, src, dst, blocks, window, out, block_list, row_list):
    out[...] = jnp.zeros_like(out)
    held = window.shape[0] // leaf
    gathered_blocks(leaf, lambda s: s < held, src, dst, blocks, window, out, block_list, row_list)


def outer_kernel(
    leaf, src, dst, place, blocks, window, far_u, coeffs, inner, out, block_list, row_list
):
    targets, groups, rank, elems = far_u.shape
    chips = targets // CORES
    group, chip, core = place[0], place[1], place[2]
    for other in range(CORES):
        for ahead in range(chips):
            target = lax.rem(chip + ahead, chips) * CORES + (core ^ other)
            bases = [far_u[target, lax.rem(group + s, groups)] for s in range(groups)]
            parts = [coeffs[s, target] for s in range(groups)]
            rows = pl.ds((other * chips + ahead) * elems, elems)
            out[rows, :] = inner[rows, :] + lax.dot_general(
                jnp.concatenate(bases, axis=0),
                jnp.concatenate(parts, axis=0),
                (((0,), (0,)), ((), ())),
                preferred_element_type=jnp.float32,
            )
    held = window.shape[0] // leaf
    gathered_blocks(leaf, lambda s: s >= held, src, dst, blocks, window, out, block_list, row_list)


VMEM = pl.BlockSpec(memory_space=pltpu.VMEM)
SMEM = pl.BlockSpec(memory_space=pltpu.SMEM)


def stress_call(kernel, rows, members, count, flops, nbytes, specs):
    return pl.pallas_call(
        kernel,
        out_shape=jax.ShapeDtypeStruct((rows, members), jnp.float32),
        in_specs=specs,
        out_specs=VMEM,
        scratch_shapes=[
            pltpu.SMEM((count + UNROLL,), jnp.int32),
            pltpu.SMEM((count + UNROLL,), jnp.int32),
        ],
        compiler_params=pltpu.CompilerParams(vmem_limit_bytes=40 * 1024 * 1024),
        cost_estimate=pl.CostEstimate(flops=flops, bytes_accessed=nbytes, transcendentals=0),
    )


def inner_stress(src, dst, blocks, window, rows):
    count, leaf, _ = blocks.shape
    members = window.shape[1]
    call = stress_call(
        functools.partial(inner_kernel, leaf),
        rows + leaf,
        members,
        count,
        2 * members * count * leaf * leaf,
        4 * rows * members,
        [SMEM, SMEM, VMEM, VMEM],
    )
    return call(src, dst, blocks, window)


def outer_stress(src, dst, place, blocks, window, far_u, coeffs, inner):
    targets, groups, rank, elems = far_u.shape
    count, leaf, _ = blocks.shape
    rows, members = inner.shape
    call = stress_call(
        functools.partial(outer_kernel, leaf),
        rows,
        members,
        count,
        members * (count * leaf * leaf + 2 * targets * groups * rank * elems),
        8 * rows * members,
        [SMEM, SMEM, SMEM, VMEM, VMEM, VMEM, VMEM, VMEM],
    )
    return call(src, dst, place, blocks, window, far_u, coeffs, inner)


def slip_rates(stress, state, load, friction_a):
    softness = friction_a[:, None]
    velocity = 2.0 * jnp.exp(-state / softness) * jnp.sinh((stress + load) / (2.0 * softness))
    speed = jnp.abs(velocity)
    drift = jnp.exp(-state) - speed / (1.0 + speed)
    return (velocity, drift)


def body(slip, state, load, friction_a, near_blocks, near_pairs, far_u, far_v, far_rank):
    elems, members = slip.shape
    leaf = near_blocks.shape[1]
    own = elems // leaf
    devices, groups = lax.axis_size("row"), lax.axis_size("clu")
    chips = devices // CORES
    clusters = devices * own
    assert REACH <= CORES * own
    group, row = lax.axis_index("clu"), lax.axis_index("row")
    chip, core = row // CORES, row % CORES
    place = jnp.stack([group, chip, core]).astype(jnp.int32)

    source = near_pairs[:, 1] - group * clusters
    before, after = source < 0, source >= clusters
    local = jnp.where(before, source + clusters, jnp.where(after, source - clusters, source))
    holder = local // own
    piece = jnp.where(
        before, (chip + 1) % chips, jnp.where(after, chip, (chip - holder // CORES + chips) % chips)
    )
    window_of = jnp.where(before | after, CORES, 0) + ((holder % CORES) ^ core)
    src = ((window_of * chips + piece) * own + local % own).astype(jnp.int32)
    target = near_pairs[:, 0] - group * clusters
    owner = target // own
    ahead = (owner // CORES - chip + chips) % chips
    dst = ((((owner % CORES) ^ core) * chips + ahead) * own + target % own).astype(jnp.int32)

    rank = far_u.shape[2]
    column = lax.broadcasted_iota(jnp.int32, (1, 1, rank, 1), 2)
    bases = jnp.where(column < far_rank[:, :, None, None], far_v, jnp.zeros_like(far_v))
    bases = [
        lax.dynamic_index_in_dim(bases, (group + s) % groups, axis=1, keepdims=False).reshape(
            devices * rank, elems
        )
        for s in range(groups)
    ]

    def with_mate(pieces):
        both = jnp.stack(pieces)
        return jnp.stack([both, core_swap(both)]).reshape(-1, members)

    def section_stress(field):
        half = field.astype(jnp.bfloat16)
        near = [half] + [chip_shift(half, s) for s in range(1, chips)]
        column = [half] + [group_shift(half, -s) for s in range(1, groups)]
        straight = jnp.where(chip == chips - 1, column[groups - 1], column[1])
        ends = [straight] + [chip_shift(straight, s) for s in range(1, chips)]
        inner = inner_stress(src, dst, near_blocks, with_mate(near), devices * elems)
        coeffs = [
            jnp.dot(bases[s], column[s], preferred_element_type=jnp.float32)
            .astype(jnp.bfloat16)
            .reshape(devices, rank, members)
            for s in range(groups)
        ]
        partial = outer_stress(
            src, dst, place, near_blocks, with_mate(ends), far_u, jnp.stack(coeffs), inner
        )
        partial = partial[: devices * elems].reshape(CORES, chips, elems, members)
        joined = [partial[0, s] + core_swap(partial[1, s]) for s in range(chips)]
        total = joined[0]
        for s in range(1, chips):
            total = total + chip_shift(joined[s].astype(jnp.bfloat16), s).astype(jnp.float32)
        return total

    velocity_one, drift_one = slip_rates(section_stress(slip), state, load, friction_a)
    slip_mid = slip + STEP * velocity_one
    state_mid = state + STEP * drift_one
    velocity_two, drift_two = slip_rates(section_stress(slip_mid), state_mid, load, friction_a)
    slip_next = slip + 0.5 * STEP * (velocity_one + velocity_two)
    state_next = state + 0.5 * STEP * (drift_one + drift_two)
    return (slip_next, state_next)


def solution(mesh):
    placed = (
        P(("grp", "clu", "row"), None),
        P(("grp", "clu", "row"), None),
        P(("grp", "clu", "row"), None),
        P(("grp", "clu", "row")),
        P(("grp", "clu", "row"), None, None),
        P(("grp", "clu", "row"), None),
        P(("grp", "clu", "row"), None, None, None),
        P(("grp", "clu", "row"), None, None, None),
        P(("grp", "clu", "row"), None),
    )
    return jax.shard_map(
        body,
        mesh=mesh,
        in_specs=placed,
        out_specs=(P(("grp", "clu", "row"), None), P(("grp", "clu", "row"), None)),
        check_vma=False,
    )
```

```python
import functools

import jax
import jax.numpy as jnp
from jax import lax
from jax.experimental import pallas as pl
from jax.experimental.pallas import tpu as pltpu
from jax.sharding import PartitionSpec as P

REACH = 4
CORES = 2
STEP = 0.2
WIDTH = 4


def core_swap(array):
    devices = lax.axis_size("row")
    return lax.ppermute(array, "row", [(i, i ^ 1) for i in range(devices)])


def chip_shift(array, step):
    devices = lax.axis_size("row")
    pairs = [(i, (i + CORES * step) % devices) for i in range(devices)]
    return lax.ppermute(array, "row", pairs)


def group_shift(array, step):
    groups = lax.axis_size("clu")
    return lax.ppermute(array, "clu", [(i, (i + step) % groups) for i in range(groups)])


def end_shift(array, step):
    devices, groups = lax.axis_size("row"), lax.axis_size("clu")
    pairs = []
    for c in range(groups):
        for r in range(devices):
            to = c + step if r >= devices - CORES else c - step
            pairs.append((c * devices + r, to % groups * devices + r))
    return lax.ppermute(array, ("clu", "row"), pairs)


def plan_kernel(leaf, spare, src, dst, plan, rows, free):
    places, chunks, targets = plan.shape[1], rows.shape[0], free.shape[0]
    for t in range(targets):
        free[t] = 0
    for i in range(places):
        plan[0, i] = 0
        plan[1, i] = spare
    for i in range(chunks):
        rows[i] = 0

    def put(j, used):
        target = dst[j]
        at = free[target]
        full = (at & (WIDTH - 1)) == 0
        at = jnp.where(full, used * WIDTH, at)
        free[target] = at + 1
        plan[0, at] = j
        plan[1, at] = src[j] * leaf
        rows[lax.shift_right_logical(at, WIDTH.bit_length() - 1)] = target * leaf
        return used + full.astype(jnp.int32)

    lax.fori_loop(0, src.shape[0], put, jnp.int32(0), unroll=4)


def stress_kernel(leaf, groups, place, plan, rows, ranks, blocks, window, far_u, far_v, *rest):
    columns, (out, coeffs) = rest[:groups], rest[groups:]
    targets, _, rank, elems = far_u.shape
    chips, members = targets // CORES, window.shape[1]
    chip, core = place[0], place[1]
    row = lax.broadcasted_iota(jnp.int32, (rank, members), 0)
    for s in range(groups):
        source = place[2 + s]
        product = jnp.dot(
            jnp.concatenate([far_v[t, source] for t in range(targets)], axis=0),
            columns[s][...],
            preferred_element_type=jnp.float32,
        )
        for t in range(targets):
            part = product[t * rank : (t + 1) * rank]
            part = jnp.where(row < ranks[t, source], part, 0.0)
            coeffs[t, s * rank : (s + 1) * rank, :] = part.astype(jnp.bfloat16)
    for other in range(CORES):
        for ahead in range(chips):
            target = lax.rem(chip + ahead, chips) * CORES + (core ^ other)
            out[pl.ds((other * chips + ahead) * elems, elems), :] = lax.dot_general(
                jnp.concatenate([far_u[target, place[2 + s]] for s in range(groups)], axis=0),
                coeffs[target],
                (((0,), (0,)), ((), ())),
                preferred_element_type=jnp.float32,
            )
    products = []
    for i in range(rows.shape[0]):
        places = range(i * WIDTH, (i + 1) * WIDTH)
        sources = [pl.ds(pl.multiple_of(plan[1, p], leaf), leaf) for p in places]
        products.append(
            jnp.dot(
                jnp.concatenate([blocks[plan[0, p]] for p in places], axis=1),
                jnp.concatenate([window[source, :] for source in sources], axis=0),
                preferred_element_type=jnp.float32,
            )
        )
    for i in range(rows.shape[0]):
        out[pl.ds(pl.multiple_of(rows[i], leaf), leaf), :] += products[i]


VMEM = pl.BlockSpec(memory_space=pltpu.VMEM)
SMEM = pl.BlockSpec(memory_space=pltpu.SMEM)
PARAMS = pltpu.CompilerParams(vmem_limit_bytes=16 * 1024 * 1024)


def planned_blocks(src, dst, leaf, targets, spare):
    chunks = (src.shape[0] + targets * (WIDTH - 1)) // WIDTH
    return pl.pallas_call(
        functools.partial(plan_kernel, leaf, spare),
        out_shape=(
            jax.ShapeDtypeStruct((2, chunks * WIDTH), jnp.int32),
            jax.ShapeDtypeStruct((chunks,), jnp.int32),
        ),
        in_specs=[SMEM, SMEM],
        out_specs=(SMEM, SMEM),
        scratch_shapes=[pltpu.SMEM((targets,), jnp.int32)],
        compiler_params=PARAMS,
        cost_estimate=pl.CostEstimate(flops=1024, bytes_accessed=1024, transcendentals=0),
    )(src, dst)


def partial_stress(place, plan, ranks, blocks, window, far_u, far_v, columns):
    targets, groups, rank, elems = far_u.shape
    count, leaf, _ = blocks.shape
    rows, members = targets * elems, window.shape[1]
    return pl.pallas_call(
        functools.partial(stress_kernel, leaf, groups),
        out_shape=jax.ShapeDtypeStruct((rows, members), jnp.float32),
        in_specs=[SMEM] * 4 + [VMEM] * (4 + groups),
        out_specs=VMEM,
        scratch_shapes=[pltpu.VMEM((targets, groups * rank, members), jnp.bfloat16)],
        compiler_params=PARAMS,
        cost_estimate=pl.CostEstimate(
            flops=2 * members * (count * leaf * leaf + 2 * targets * groups * rank * elems),
            bytes_accessed=4 * rows * members,
            transcendentals=0,
        ),
    )(place, plan[0], plan[1], ranks, blocks, window, far_u, far_v, *columns)


def slip_rates(stress, state, load, friction_a):
    softness = friction_a[:, None]
    velocity = 2.0 * jnp.exp(-state / softness) * jnp.sinh((stress + load) / (2.0 * softness))
    speed = jnp.abs(velocity)
    drift = jnp.exp(-state) - speed / (1.0 + speed)
    return (velocity, drift)


def body(slip, state, load, friction_a, near_blocks, near_pairs, far_u, far_v, far_rank):
    elems, members = slip.shape
    leaf = near_blocks.shape[1]
    own = elems // leaf
    devices, groups = lax.axis_size("row"), lax.axis_size("clu")
    chips = devices // CORES
    clusters = devices * own
    assert REACH <= CORES * own
    group, row = lax.axis_index("clu"), lax.axis_index("row")
    chip, core = row // CORES, row % CORES
    toward = jnp.where(chip == chips - 1, -1, 1)
    sources = [group]
    for s in range(1, groups):
        sources.append(group + (toward if s % 2 else -toward) * ((s + 1) // 2))
    sources = [(source + groups) % groups for source in sources]
    place = jnp.stack([chip, core] + sources).astype(jnp.int32)

    source = near_pairs[:, 1] - group * clusters
    before, after = source < 0, source >= clusters
    local = jnp.where(before, source + clusters, jnp.where(after, source - clusters, source))
    holder = local // own
    piece = jnp.where(
        before, (chip + 1) % chips, jnp.where(after, chip, (chip - holder // CORES + chips) % chips)
    )
    piece = piece + jnp.where(before | after, chips, 0)
    src = ((((holder % CORES) ^ core) * 2 * chips + piece) * own + local % own).astype(jnp.int32)
    target = near_pairs[:, 0] - group * clusters
    owner = target // own
    ahead = (owner // CORES - chip + chips) % chips
    dst = ((((owner % CORES) ^ core) * chips + ahead) * own + target % own).astype(jnp.int32)

    plan = planned_blocks(src, dst, leaf, clusters, 4 * chips * elems)
    spare = jnp.zeros((leaf, members), jnp.bfloat16)

    def section_stress(field):
        half = field.astype(jnp.bfloat16)
        straight = end_shift(half, 1)
        near = jnp.concatenate([half] + [chip_shift(half, s) for s in range(1, chips)])
        column = [half, straight, end_shift(half, -1)]
        while len(column) < groups:
            step = 1 if len(column) % 2 else -1
            column.append(end_shift(column[-2], step))
        ends = jnp.concatenate([straight] + [chip_shift(straight, s) for s in range(1, chips)])
        window = jnp.concatenate([near, ends, core_swap(near), core_swap(ends), spare])
        partial = partial_stress(place, plan, far_rank, near_blocks, window, far_u, far_v, column)
        partial = partial.reshape(CORES, chips, elems, members)
        joined = [partial[0, s] + core_swap(partial[1, s]) for s in range(chips)]
        total = joined[0]
        for s in range(1, chips):
            total = total + chip_shift(joined[s].astype(jnp.bfloat16), s).astype(jnp.float32)
        return total

    velocity_one, drift_one = slip_rates(section_stress(slip), state, load, friction_a)
    slip_mid = slip + STEP * velocity_one
    state_mid = state + STEP * drift_one
    velocity_two, drift_two = slip_rates(section_stress(slip_mid), state_mid, load, friction_a)
    slip_next = slip + 0.5 * STEP * (velocity_one + velocity_two)
    state_next = state + 0.5 * STEP * (drift_one + drift_two)
    return (slip_next, state_next)


def solution(mesh):
    placed = (
        P(("grp", "clu", "row"), None),
        P(("grp", "clu", "row"), None),
        P(("grp", "clu", "row"), None),
        P(("grp", "clu", "row")),
        P(("grp", "clu", "row"), None, None),
        P(("grp", "clu", "row"), None),
        P(("grp", "clu", "row"), None, None, None),
        P(("grp", "clu", "row"), None, None, None),
        P(("grp", "clu", "row"), None),
    )
    return jax.shard_map(
        body,
        mesh=mesh,
        in_specs=placed,
        out_specs=(P(("grp", "clu", "row"), None), P(("grp", "clu", "row"), None)),
        check_vma=False,
    )
```

```python
import functools

import jax
import jax.numpy as jnp
from jax import lax
from jax.experimental import pallas as pl
from jax.experimental.pallas import tpu as pltpu
from jax.sharding import PartitionSpec as P

REACH = 4
CORES = 2
STEP = 0.2
WIDTH = 4


def core_swap(array):
    devices = lax.axis_size("row")
    return lax.ppermute(array, "row", [(i, i ^ 1) for i in range(devices)])


def chip_shift(array, step):
    devices = lax.axis_size("row")
    pairs = [(i, (i + CORES * step) % devices) for i in range(devices)]
    return lax.ppermute(array, "row", pairs)


def group_shift(array, step):
    groups = lax.axis_size("clu")
    return lax.ppermute(array, "clu", [(i, (i + step) % groups) for i in range(groups)])


def end_shift(array, step):
    devices, groups = lax.axis_size("row"), lax.axis_size("clu")
    pairs = []
    for c in range(groups):
        for r in range(devices):
            to = c + step if r >= devices - CORES else c - step
            pairs.append((c * devices + r, to % groups * devices + r))
    return lax.ppermute(array, ("clu", "row"), pairs)


def around(value, size):
    value = jnp.where(value < 0, value + size, value)
    return jnp.where(value >= size, value - size, value)


def here():
    row = lax.axis_index("row")
    return lax.axis_index("clu"), lax.div(row, CORES), lax.rem(row, CORES)


def plan_kernel(leaf, own, pairs, plan, rows, free, source_rows, target_rows):
    devices = lax.axis_size("row")
    chips, clusters = devices // CORES, devices * own
    group, chip, core = here()
    for near in range(-REACH, clusters + REACH):
        holder = near % clusters // own
        if near < 0:
            piece = chips + around(chip + 1, chips)
        elif near >= clusters:
            piece = chips + chip
        else:
            piece = around(chip - holder // CORES, chips)
        piece = ((core ^ (holder % CORES)) * 2 * chips + piece) * own + near % own
        source_rows[near + REACH] = piece * leaf
    for target in range(clusters):
        owner = target // own
        piece = (core ^ (owner % CORES)) * chips + around(owner // CORES - chip, chips)
        target_rows[target] = (piece * own + target % own) * leaf
        free[target] = 0
    for i in range(plan.shape[1]):
        plan[0, i] = 0
        plan[1, i] = 4 * chips * own * leaf
    for i in range(rows.shape[0]):
        rows[i] = 0

    def put(j, used):
        target = pairs[0, j] - group * clusters
        at = free[target]
        full = (at & (WIDTH - 1)) == 0
        at = jnp.where(full, used * WIDTH, at)
        free[target] = at + 1
        plan[0, at] = j
        plan[1, at] = source_rows[pairs[1, j] - group * clusters + REACH]
        rows[lax.shift_right_logical(at, WIDTH.bit_length() - 1)] = target_rows[target]
        return used + full.astype(jnp.int32)

    lax.fori_loop(0, pairs.shape[1], put, jnp.int32(0), unroll=4)


def stress_kernel(leaf, plan, rows, ranks, blocks, window, far_u, far_v, *rest):
    targets, groups, rank, elems = far_u.shape
    columns, (out, coeffs) = rest[:groups], rest[groups:]
    chips, members = targets // CORES, window.shape[1]
    group, chip, core = here()
    toward = jnp.where(chip == chips - 1, -1, 1)
    steps = [(s + 1) // 2 if s % 2 else -(s // 2) for s in range(groups)]
    sources = [around(group + toward * step, groups) for step in steps]
    row = lax.broadcasted_iota(jnp.int32, (rank, members), 0)
    for s in range(groups):
        source = sources[s]
        product = jnp.dot(
            jnp.concatenate([far_v[t, source] for t in range(targets)], axis=0),
            columns[s][...],
            preferred_element_type=jnp.float32,
        )
        for t in range(targets):
            part = product[t * rank : (t + 1) * rank]
            part = jnp.where(row < ranks[t, source], part, 0.0)
            coeffs[t, s * rank : (s + 1) * rank, :] = part.astype(jnp.bfloat16)
    for other in range(CORES):
        for ahead in range(chips):
            target = around(chip + ahead, chips) * CORES + (core ^ other)
            out[pl.ds((other * chips + ahead) * elems, elems), :] = lax.dot_general(
                jnp.concatenate([far_u[target, source] for source in sources], axis=0),
                coeffs[target],
                (((0,), (0,)), ((), ())),
                preferred_element_type=jnp.float32,
            )
    products = []
    for i in range(rows.shape[0]):
        places = range(i * WIDTH, (i + 1) * WIDTH)
        sources = [pl.ds(pl.multiple_of(plan[1, p], leaf), leaf) for p in places]
        products.append(
            jnp.dot(
                jnp.concatenate([blocks[plan[0, p]] for p in places], axis=1),
                jnp.concatenate([window[source, :] for source in sources], axis=0),
                preferred_element_type=jnp.float32,
            )
        )
    for i in range(rows.shape[0]):
        out[pl.ds(pl.multiple_of(rows[i], leaf), leaf), :] += products[i]


VMEM = pl.BlockSpec(memory_space=pltpu.VMEM)
SMEM = pl.BlockSpec(memory_space=pltpu.SMEM)
PARAMS = pltpu.CompilerParams(vmem_limit_bytes=16 * 1024 * 1024)


def planned_blocks(pairs, leaf, own):
    targets = lax.axis_size("row") * own
    chunks = (pairs.shape[1] + targets * (WIDTH - 1)) // WIDTH
    return pl.pallas_call(
        functools.partial(plan_kernel, leaf, own),
        out_shape=(
            jax.ShapeDtypeStruct((2, chunks * WIDTH), jnp.int32),
            jax.ShapeDtypeStruct((chunks,), jnp.int32),
        ),
        in_specs=[SMEM],
        out_specs=(SMEM, SMEM),
        scratch_shapes=[
            pltpu.SMEM((targets,), jnp.int32),
            pltpu.SMEM((targets + 2 * REACH,), jnp.int32),
            pltpu.SMEM((targets,), jnp.int32),
        ],
        compiler_params=PARAMS,
        cost_estimate=pl.CostEstimate(flops=4_000_000_000, bytes_accessed=10_000_000, transcendentals=0),
    )(pairs)


def partial_stress(plan, ranks, blocks, window, far_u, far_v, columns):
    targets, groups, rank, elems = far_u.shape
    count, leaf, _ = blocks.shape
    rows, members = targets * elems, window.shape[1]
    return pl.pallas_call(
        functools.partial(stress_kernel, leaf),
        out_shape=jax.ShapeDtypeStruct((rows, members), jnp.float32),
        in_specs=[SMEM] * 3 + [VMEM] * (4 + groups),
        out_specs=VMEM,
        scratch_shapes=[pltpu.VMEM((targets, groups * rank, members), jnp.bfloat16)],
        compiler_params=PARAMS,
        cost_estimate=pl.CostEstimate(
            flops=2 * members * (count * leaf * leaf + 2 * targets * groups * rank * elems),
            bytes_accessed=4 * rows * members,
            transcendentals=0,
        ),
    )(plan[0], plan[1], ranks, blocks, window, far_u, far_v, *columns)


def slip_rates(stress, state, load, friction_a):
    softness = friction_a[:, None]
    velocity = 2.0 * jnp.exp(-state / softness) * jnp.sinh((stress + load) / (2.0 * softness))
    speed = jnp.abs(velocity)
    drift = jnp.exp(-state) - speed / (1.0 + speed)
    return (velocity, drift)


def body(slip, state, load, friction_a, near_blocks, near_pairs, far_u, far_v, far_rank):
    elems, members = slip.shape
    leaf = near_blocks.shape[1]
    own = elems // leaf
    devices, groups = lax.axis_size("row"), lax.axis_size("clu")
    chips = devices // CORES
    assert REACH <= CORES * own
    spare = jnp.zeros((leaf, members), jnp.bfloat16)
    plans = []

    def planned(after):
        if not plans:
            after, pairs = lax.optimization_barrier((after, near_pairs.T))
            plans.append(planned_blocks(pairs, leaf, own))
        return after, plans[0]

    def section_stress(field):
        half = field.astype(jnp.bfloat16)
        straight = end_shift(half, 1)
        straight, plan = planned(straight)
        near = jnp.concatenate([half] + [chip_shift(half, s) for s in range(1, chips)])
        column = [half, straight, end_shift(half, -1)]
        while len(column) < groups:
            column.append(end_shift(column[-2], 1 if len(column) % 2 else -1))
        ends = [chip_shift(straight, s) for s in range(1, chips)]
        ends, plan = lax.optimization_barrier((ends, plan))
        ends = jnp.concatenate([straight] + ends)
        window = jnp.concatenate([near, ends, core_swap(near), core_swap(ends), spare])
        partial = partial_stress(plan, far_rank, near_blocks, window, far_u, far_v, column)
        partial = partial.reshape(CORES, chips, elems, members)
        joined = [partial[0, s] + core_swap(partial[1, s]) for s in range(chips)]
        total = joined[0]
        for s in range(1, chips):
            total = total + chip_shift(joined[s].astype(jnp.bfloat16), s).astype(jnp.float32)
        return total

    velocity_one, drift_one = slip_rates(section_stress(slip), state, load, friction_a)
    slip_mid = slip + STEP * velocity_one
    state_mid = state + STEP * drift_one
    velocity_two, drift_two = slip_rates(section_stress(slip_mid), state_mid, load, friction_a)
    slip_next = slip + 0.5 * STEP * (velocity_one + velocity_two)
    state_next = state + 0.5 * STEP * (drift_one + drift_two)
    return (slip_next, state_next)


def solution(mesh):
    placed = (
        P(("grp", "clu", "row"), None),
        P(("grp", "clu", "row"), None),
        P(("grp", "clu", "row"), None),
        P(("grp", "clu", "row")),
        P(("grp", "clu", "row"), None, None),
        P(("grp", "clu", "row"), None),
        P(("grp", "clu", "row"), None, None, None),
        P(("grp", "clu", "row"), None, None, None),
        P(("grp", "clu", "row"), None),
    )
    return jax.shard_map(
        body,
        mesh=mesh,
        in_specs=placed,
        out_specs=(P(("grp", "clu", "row"), None), P(("grp", "clu", "row"), None)),
        check_vma=False,
    )
```

```python
import functools

import jax
import jax.numpy as jnp
from jax import lax
from jax.experimental import pallas as pl
from jax.experimental.pallas import tpu as pltpu
from jax.sharding import PartitionSpec as P

REACH = 4
CORES = 2
STEP = 0.2
LOG_TWO = 0.6931471805599453
WIDTH = 4


def core_swap(array):
    devices = lax.axis_size("row")
    return lax.ppermute(array, "row", [(i, i ^ 1) for i in range(devices)])


def chip_shift(array, step):
    devices = lax.axis_size("row")
    pairs = [(i, (i + CORES * step) % devices) for i in range(devices)]
    return lax.ppermute(array, "row", pairs)


def group_shift(array, step):
    groups = lax.axis_size("clu")
    return lax.ppermute(array, "clu", [(i, (i + step) % groups) for i in range(groups)])


def end_shift(array, step):
    devices, groups = lax.axis_size("row"), lax.axis_size("clu")
    pairs = []
    for c in range(groups):
        for r in range(devices):
            to = c + step if r >= devices - CORES else c - step
            pairs.append((c * devices + r, to % groups * devices + r))
    return lax.ppermute(array, ("clu", "row"), pairs)


def around(value, size):
    value = jnp.where(value < 0, value + size, value)
    return jnp.where(value >= size, value - size, value)


def here():
    row = lax.axis_index("row")
    return lax.axis_index("clu"), lax.div(row, CORES), lax.rem(row, CORES)


def plan_kernel(leaf, own, pairs, plan, rows, free, source_rows, target_rows):
    devices = lax.axis_size("row")
    chips, clusters = devices // CORES, devices * own
    group, chip, core = here()
    for near in range(-REACH, clusters + REACH):
        holder = near % clusters // own
        if near < 0:
            piece = chips + around(chip + 1, chips)
        elif near >= clusters:
            piece = chips + chip
        else:
            piece = around(chip - holder // CORES, chips)
        piece = ((core ^ (holder % CORES)) * 2 * chips + piece) * own + near % own
        source_rows[near + REACH] = piece * leaf
    for target in range(clusters):
        owner = target // own
        piece = (core ^ (owner % CORES)) * chips + around(owner // CORES - chip, chips)
        target_rows[target] = (piece * own + target % own) * leaf
        free[target] = 0
    for i in range(plan.shape[1]):
        plan[0, i] = 0
        plan[1, i] = 4 * chips * own * leaf
    for i in range(rows.shape[0]):
        rows[i] = 0

    def put(j, used):
        target = pairs[0, j] - group * clusters
        at = free[target]
        full = (at & (WIDTH - 1)) == 0
        at = jnp.where(full, used * WIDTH, at)
        free[target] = at + 1
        plan[0, at] = j
        plan[1, at] = source_rows[pairs[1, j] - group * clusters + REACH]
        rows[lax.shift_right_logical(at, WIDTH.bit_length() - 1)] = target_rows[target]
        return used + full.astype(jnp.int32)

    lax.fori_loop(0, pairs.shape[1], put, jnp.int32(0), unroll=8)


def stress_kernel(leaf, plan, rows, blocks, window, far_u, far_v, *rest):
    targets, elems, ranks = far_u.shape
    groups, rank = far_v.shape[0], far_v.shape[1] // targets
    columns, out = rest[:groups], rest[groups]
    coeffs = [
        jnp.dot(far_v[s], columns[s][...], preferred_element_type=jnp.float32).astype(jnp.bfloat16)
        for s in range(groups)
    ]
    for t in range(targets):
        out[pl.ds(t * elems, elems), :] = jnp.dot(
            far_u[t],
            jnp.concatenate([c[t * rank : (t + 1) * rank] for c in coeffs], axis=0),
            preferred_element_type=jnp.float32,
        )
    products = []
    for i in range(rows.shape[0]):
        places = range(i * WIDTH, (i + 1) * WIDTH)
        sources = [pl.ds(pl.multiple_of(plan[1, p], leaf), leaf) for p in places]
        products.append(
            jnp.dot(
                jnp.concatenate([blocks[plan[0, p]] for p in places], axis=1),
                jnp.concatenate([window[source, :] for source in sources], axis=0),
                preferred_element_type=jnp.float32,
            )
        )
    for i in range(rows.shape[0]):
        out[pl.ds(pl.multiple_of(rows[i], leaf), leaf), :] += products[i]


def bases_kernel(ranks, far_u, far_v, by_target, by_source):
    targets, groups, rank, elems = far_u.shape
    chips = targets // CORES
    group, chip, core = here()
    toward = jnp.where(chip == chips - 1, -1, 1)
    steps = [(s + 1) // 2 if s % 2 else -(s // 2) for s in range(groups)]
    sources = [around(group + toward * step, groups) for step in steps]
    row = lax.broadcasted_iota(jnp.int32, (rank, elems), 0)
    for t in range(targets):
        other, ahead = t // chips, t % chips
        target = around(chip + ahead, chips) * CORES + (core ^ other)
        for s, source in enumerate(sources):
            kept = jnp.where(row < ranks[target, source], far_v[target, source].astype(jnp.float32), 0.0)
            by_source[s, t * rank : (t + 1) * rank, :] = kept.astype(jnp.bfloat16)
        bases = jnp.concatenate([far_u[target, source] for source in sources], axis=0)
        by_target[t] = bases.astype(jnp.float32).T.astype(jnp.bfloat16)


def finish_kernel(near, mate, received, scale, shift, weight, slip, state, slip_out, state_out):
    stress = near[...] + mate[...]
    for s in range(received.shape[0]):
        stress = stress + received[s].astype(jnp.float32)
    halved = stress * scale[...] + shift[...]
    velocity = weight[...] * (jnp.exp(halved - LOG_TWO) - jnp.exp(-halved - LOG_TWO))
    speed = jnp.abs(velocity)
    slip_out[...] = slip[...] + 0.5 * STEP * velocity
    state_out[...] = state[...] - 0.5 * STEP * (speed / (1.0 + speed))


VMEM = pl.BlockSpec(memory_space=pltpu.VMEM)
SMEM = pl.BlockSpec(memory_space=pltpu.SMEM)
PARAMS = pltpu.CompilerParams(vmem_limit_bytes=16 * 1024 * 1024)


def planned_blocks(pairs, leaf, own):
    targets = lax.axis_size("row") * own
    chunks = (pairs.shape[1] + targets * (WIDTH - 1)) // WIDTH
    return pl.pallas_call(
        functools.partial(plan_kernel, leaf, own),
        out_shape=(
            jax.ShapeDtypeStruct((2, chunks * WIDTH), jnp.int32),
            jax.ShapeDtypeStruct((chunks,), jnp.int32),
        ),
        in_specs=[SMEM],
        out_specs=(SMEM, SMEM),
        scratch_shapes=[
            pltpu.SMEM((targets,), jnp.int32),
            pltpu.SMEM((targets + 2 * REACH,), jnp.int32),
            pltpu.SMEM((targets,), jnp.int32),
        ],
        compiler_params=PARAMS,
        cost_estimate=pl.CostEstimate(flops=4_000_000_000, bytes_accessed=10_000_000, transcendentals=0),
    )(pairs)


def arranged_bases(ranks, far_u, far_v):
    targets, groups, rank, elems = far_u.shape
    return pl.pallas_call(
        bases_kernel,
        out_shape=(
            jax.ShapeDtypeStruct((targets, elems, groups * rank), jnp.bfloat16),
            jax.ShapeDtypeStruct((groups, targets * rank, elems), jnp.bfloat16),
        ),
        in_specs=[SMEM, VMEM, VMEM],
        out_specs=(VMEM, VMEM),
        compiler_params=PARAMS,
        cost_estimate=pl.CostEstimate(flops=1024, bytes_accessed=1_000_000, transcendentals=0),
    )(ranks, far_u, far_v)


def partial_stress(plan, blocks, window, far_u, far_v, columns):
    targets, elems, ranks = far_u.shape
    count, leaf, _ = blocks.shape
    members, groups = window.shape[1], len(columns)
    return pl.pallas_call(
        functools.partial(stress_kernel, leaf),
        out_shape=jax.ShapeDtypeStruct((targets * elems, members), jnp.float32),
        in_specs=[SMEM] * 2 + [VMEM] * (4 + groups),
        out_specs=VMEM,
        compiler_params=PARAMS,
        cost_estimate=pl.CostEstimate(
            flops=2 * members * (count * leaf * leaf + 2 * targets * ranks * elems),
            bytes_accessed=4 * targets * elems * members,
            transcendentals=0,
        ),
    )(plan[0], plan[1], blocks, window, far_u, far_v, *columns)


def slip_rates(stress, state, load, friction_a):
    softness = friction_a[:, None]
    halved = (stress + load) / (2.0 * softness)
    growth = jnp.exp(halved - LOG_TWO) - jnp.exp(-halved - LOG_TWO)
    velocity = 2.0 * jnp.exp(-state / softness) * growth
    speed = jnp.abs(velocity)
    drift = jnp.exp(-state) - speed / (1.0 + speed)
    return (velocity, drift)


def body(slip, state, load, friction_a, near_blocks, near_pairs, far_u, far_v, far_rank):
    elems, members = slip.shape
    leaf = near_blocks.shape[1]
    own = elems // leaf
    devices, groups = lax.axis_size("row"), lax.axis_size("clu")
    chips = devices // CORES
    assert REACH <= CORES * own
    spare = jnp.zeros((leaf, members), jnp.bfloat16)
    plans = []

    def planned(after):
        if not plans:
            pairs = near_pairs.T
            after, *tables = lax.optimization_barrier((after, far_rank, far_u, far_v))
            plans.append((planned_blocks(pairs, leaf, own), arranged_bases(*tables)))
        return after, plans[0]

    def section_stress(field):
        half = field.astype(jnp.bfloat16)
        straight = end_shift(half, 1)
        straight, (plan, bases) = planned(straight)
        near = jnp.concatenate([half] + [chip_shift(half, s) for s in range(1, chips)])
        column = [half, straight, end_shift(half, -1)]
        while len(column) < groups:
            column.append(end_shift(column[-2], 1 if len(column) % 2 else -1))
        ends = [chip_shift(straight, s) for s in range(1, chips)]
        ends, plan, bases = lax.optimization_barrier((ends, plan, bases))
        ends = jnp.concatenate([straight] + ends)
        others = [core_swap(near[:elems]), core_swap(near[elems:])]
        window = jnp.concatenate([near, ends] + others + [core_swap(ends), spare])
        partial = partial_stress(plan, near_blocks, window, *bases, column)
        partial = partial.reshape(CORES, chips, elems, members)
        joined = [core_swap(partial[1, s]) for s in range(chips)]
        sent = [(partial[0, s] + joined[s]).astype(jnp.bfloat16) for s in range(1, chips)]
        return partial[0, 0], joined[0], [chip_shift(sent[s - 1], s) for s in range(1, chips)]

    near, mate, received = section_stress(slip)
    stress_one = near + mate
    for part in received:
        stress_one = stress_one + part.astype(jnp.float32)
    velocity_one, drift_one = slip_rates(stress_one, state, load, friction_a)
    slip_mid = slip + STEP * velocity_one
    near, mate, received = section_stress(slip_mid)

    state_mid = state + STEP * drift_one
    softness = friction_a[:, None]
    scale = jnp.broadcast_to(1.0 / (2.0 * softness), slip.shape)
    shift = load * scale
    weight = 2.0 * jnp.exp(-state_mid / softness)
    slip_most = slip + 0.5 * STEP * velocity_one
    state_most = state + 0.5 * STEP * (drift_one + jnp.exp(-state_mid))
    return pl.pallas_call(
        finish_kernel,
        out_shape=(
            jax.ShapeDtypeStruct(slip.shape, jnp.float32),
            jax.ShapeDtypeStruct(slip.shape, jnp.float32),
        ),
        in_specs=[VMEM] * 8,
        out_specs=(VMEM, VMEM),
        compiler_params=PARAMS,
        cost_estimate=pl.CostEstimate(
            flops=16 * slip.size, bytes_accessed=32 * slip.size, transcendentals=2 * slip.size
        ),
    )(near, mate, jnp.stack(received), scale, shift, weight, slip_most, state_most)


def solution(mesh):
    placed = (
        P(("grp", "clu", "row"), None),
        P(("grp", "clu", "row"), None),
        P(("grp", "clu", "row"), None),
        P(("grp", "clu", "row")),
        P(("grp", "clu", "row"), None, None),
        P(("grp", "clu", "row"), None),
        P(("grp", "clu", "row"), None, None, None),
        P(("grp", "clu", "row"), None, None, None),
        P(("grp", "clu", "row"), None),
    )
    return jax.shard_map(
        body,
        mesh=mesh,
        in_specs=placed,
        out_specs=(P(("grp", "clu", "row"), None), P(("grp", "clu", "row"), None)),
        check_vma=False,
    )
```

```python
import functools

import jax
import jax.numpy as jnp
from jax import lax
from jax.experimental import pallas as pl
from jax.experimental.pallas import tpu as pltpu
from jax.sharding import PartitionSpec as P

REACH = 4
CORES = 2
STEP = 0.2
LOG_TWO = 0.6931471805599453
WIDTH = 4
PARTS = 4


def core_swap(array):
    devices = lax.axis_size("row")
    return lax.ppermute(array, "row", [(i, i ^ 1) for i in range(devices)])


def chip_shift(array, step):
    devices = lax.axis_size("row")
    pairs = [(i, (i + CORES * step) % devices) for i in range(devices)]
    return lax.ppermute(array, "row", pairs)


def group_shift(array, step):
    groups = lax.axis_size("clu")
    return lax.ppermute(array, "clu", [(i, (i + step) % groups) for i in range(groups)])


def end_shift(array, step):
    devices, groups = lax.axis_size("row"), lax.axis_size("clu")
    pairs = []
    for c in range(groups):
        for r in range(devices):
            to = c + step if r >= devices - CORES else c - step
            pairs.append((c * devices + r, to % groups * devices + r))
    return lax.ppermute(array, ("clu", "row"), pairs)


def around(value, size):
    value = jnp.where(value < 0, value + size, value)
    return jnp.where(value >= size, value - size, value)


def here():
    row = lax.axis_index("row")
    return lax.axis_index("clu"), lax.div(row, CORES), lax.rem(row, CORES)


def plan_kernel(leaf, own, pairs, plan, free, source_rows, target_rows):
    devices = lax.axis_size("row")
    chips, clusters = devices // CORES, devices * own
    group, chip, core = here()
    for near in range(-REACH, clusters + REACH):
        holder = near % clusters // own
        if near < 0:
            piece = chips + around(chip + 1, chips)
        elif near >= clusters:
            piece = chips + chip
        else:
            piece = around(chip - holder // CORES, chips)
        piece = ((core ^ (holder % CORES)) * 2 * chips + piece) * own + near % own
        source_rows[near + REACH] = piece * leaf
    for target in range(clusters):
        owner = target // own
        piece = (core ^ (owner % CORES)) * chips + around(owner // CORES - chip, chips)
        target_rows[target] = (piece * own + target % own) * leaf
        free[target] = 0
    for i in range(plan.shape[1]):
        plan[0, i] = 0
        plan[1, i] = 4 * chips * own * leaf
        plan[2, i] = 0

    def put(j, used):
        target = pairs[0, j] - group * clusters
        at = free[target]
        full = (at & (WIDTH - 1)) == 0
        at = jnp.where(full, used * WIDTH, at)
        free[target] = at + 1
        plan[0, at] = j
        plan[1, at] = source_rows[pairs[1, j] - group * clusters + REACH]
        plan[2, lax.shift_right_logical(at, WIDTH.bit_length() - 1)] = target_rows[target]
        return used + full.astype(jnp.int32)

    lax.fori_loop(0, pairs.shape[1], put, jnp.int32(0), unroll=8)


def stress_kernel(leaf, plan, blocks, window, far_u, far_v, *rest):
    targets, elems, ranks = far_u.shape
    groups, rank = far_v.shape[0], far_v.shape[1] // targets
    columns, out = rest[:groups], rest[groups]
    coeffs = [
        jnp.dot(far_v[s], columns[s][...], preferred_element_type=jnp.float32).astype(jnp.bfloat16)
        for s in range(groups)
    ]
    for t in range(targets):
        out[pl.ds(t * elems, elems), :] = jnp.dot(
            far_u[t],
            jnp.concatenate([c[t * rank : (t + 1) * rank] for c in coeffs], axis=0),
            preferred_element_type=jnp.float32,
        )
    products = []
    chunks = plan.shape[1] // WIDTH
    for i in range(chunks):
        places = range(i * WIDTH, (i + 1) * WIDTH)
        sources = [pl.ds(pl.multiple_of(plan[1, p], leaf), leaf) for p in places]
        products.append(
            jnp.dot(
                jnp.concatenate([blocks[plan[0, p]] for p in places], axis=1),
                jnp.concatenate([window[source, :] for source in sources], axis=0),
                preferred_element_type=jnp.float32,
            )
        )
    for i in range(chunks):
        out[pl.ds(pl.multiple_of(plan[2, i], leaf), leaf), :] += products[i]


def bases_kernel(ranks, far_u, far_v, by_target, by_source):
    targets, groups, rank, elems = far_u.shape
    chips = targets // CORES
    group, chip, core = here()
    toward = jnp.where(chip == chips - 1, -1, 1)
    steps = [(s + 1) // 2 if s % 2 else -(s // 2) for s in range(groups)]
    sources = [around(group + toward * step, groups) for step in steps]
    row = lax.broadcasted_iota(jnp.int32, (rank, elems), 0)
    for t in range(targets):
        other, ahead = t // chips, t % chips
        target = around(chip + ahead, chips) * CORES + (core ^ other)
        for s, source in enumerate(sources):
            kept = jnp.where(row < ranks[target, source], far_v[target, source].astype(jnp.float32), 0.0)
            by_source[s, t * rank : (t + 1) * rank, :] = kept.astype(jnp.bfloat16)
        bases = jnp.concatenate([far_u[target, source] for source in sources], axis=0)
        by_target[t] = bases.astype(jnp.float32).T.astype(jnp.bfloat16)


def finish_kernel(
    near, mate, received, scale, shift, weight, slip, state, slip_out, state_out, slips, states, done
):
    parts = done.shape[0]
    size = near.shape[0] // parts
    copies = []
    for part in range(parts):
        rows = pl.ds(part * size, size)
        stress = near[rows, :] + mate[rows, :]
        for s in range(received.shape[0]):
            stress = stress + received[s, rows, :].astype(jnp.float32)
        halved = stress * scale[rows, :] + shift[rows, :]
        velocity = weight[rows, :] * (jnp.exp(halved - LOG_TWO) - jnp.exp(-halved - LOG_TWO))
        speed = jnp.abs(velocity)
        slips[rows, :] = slip[rows, :] + 0.5 * STEP * velocity
        states[rows, :] = state[rows, :] - 0.5 * STEP * (speed / (1.0 + speed))
        for at, (held, out) in enumerate(((slips, slip_out), (states, state_out))):
            copies.append(pltpu.make_async_copy(held.at[rows], out.at[rows], done.at[part, at]))
            copies[-1].start()
    for copy in copies:
        copy.wait()


VMEM = pl.BlockSpec(memory_space=pltpu.VMEM)
SMEM = pl.BlockSpec(memory_space=pltpu.SMEM)
PARAMS = pltpu.CompilerParams(vmem_limit_bytes=16 * 1024 * 1024)


def planned_blocks(pairs, leaf, own):
    targets = lax.axis_size("row") * own
    chunks = (pairs.shape[1] + targets * (WIDTH - 1)) // WIDTH
    return pl.pallas_call(
        functools.partial(plan_kernel, leaf, own),
        out_shape=jax.ShapeDtypeStruct((3, chunks * WIDTH), jnp.int32),
        in_specs=[SMEM],
        out_specs=SMEM,
        scratch_shapes=[
            pltpu.SMEM((targets,), jnp.int32),
            pltpu.SMEM((targets + 2 * REACH,), jnp.int32),
            pltpu.SMEM((targets,), jnp.int32),
        ],
        compiler_params=PARAMS,
        cost_estimate=pl.CostEstimate(flops=4_000_000_000, bytes_accessed=10_000_000, transcendentals=0),
    )(pairs)


def arranged_bases(ranks, far_u, far_v):
    targets, groups, rank, elems = far_u.shape
    return pl.pallas_call(
        bases_kernel,
        out_shape=(
            jax.ShapeDtypeStruct((targets, elems, groups * rank), jnp.bfloat16),
            jax.ShapeDtypeStruct((groups, targets * rank, elems), jnp.bfloat16),
        ),
        in_specs=[SMEM, VMEM, VMEM],
        out_specs=(VMEM, VMEM),
        compiler_params=PARAMS,
        cost_estimate=pl.CostEstimate(flops=1024, bytes_accessed=1_000_000, transcendentals=0),
    )(ranks, far_u, far_v)


def partial_stress(plan, blocks, window, far_u, far_v, columns):
    targets, elems, ranks = far_u.shape
    count, leaf, _ = blocks.shape
    members, groups = window.shape[1], len(columns)
    return pl.pallas_call(
        functools.partial(stress_kernel, leaf),
        out_shape=jax.ShapeDtypeStruct((targets * elems, members), jnp.float32),
        in_specs=[SMEM] + [VMEM] * (4 + groups),
        out_specs=VMEM,
        compiler_params=PARAMS,
        cost_estimate=pl.CostEstimate(
            flops=2 * members * (count * leaf * leaf + 2 * targets * ranks * elems),
            bytes_accessed=4 * targets * elems * members,
            transcendentals=0,
        ),
    )(plan, blocks, window, far_u, far_v, *columns)


def slip_rates(stress, state, load, friction_a):
    softness = friction_a[:, None]
    halved = (stress + load) / (2.0 * softness)
    growth = jnp.exp(halved - LOG_TWO) - jnp.exp(-halved - LOG_TWO)
    velocity = 2.0 * jnp.exp(-state / softness) * growth
    speed = jnp.abs(velocity)
    drift = jnp.exp(-state) - speed / (1.0 + speed)
    return (velocity, drift)


def body(slip, state, load, friction_a, near_blocks, near_pairs, far_u, far_v, far_rank):
    elems, members = slip.shape
    leaf = near_blocks.shape[1]
    own = elems // leaf
    devices, groups = lax.axis_size("row"), lax.axis_size("clu")
    chips = devices // CORES
    assert REACH <= CORES * own
    spare = jnp.zeros((leaf, members), jnp.bfloat16)
    plans = []

    def planned(after):
        if not plans:
            pairs = near_pairs.T
            after, *tables = lax.optimization_barrier((after, far_rank, far_u, far_v))
            plans.append((planned_blocks(pairs, leaf, own), arranged_bases(*tables)))
        return after, plans[0]

    def section_stress(field):
        half = field.astype(jnp.bfloat16)
        near = jnp.concatenate([half] + [chip_shift(half, s) for s in range(1, chips)])
        straight = end_shift(half, 1)
        straight, (plan, bases) = planned(straight)
        column = [half, straight, end_shift(half, -1)]
        while len(column) < groups:
            column.append(end_shift(column[-2], 1 if len(column) % 2 else -1))
        ends = [chip_shift(straight, s) for s in range(1, chips)]
        ends, plan, bases = lax.optimization_barrier((ends, plan, bases))
        ends = jnp.concatenate([straight] + ends)
        others = [core_swap(near[:elems]), core_swap(near[elems:])]
        window = jnp.concatenate([near, ends] + others + [core_swap(ends), spare])
        partial = partial_stress(plan, near_blocks, window, *bases, column)
        partial = partial.reshape(CORES, chips, elems, members)
        joined = [core_swap(partial[1, s]) for s in range(chips)]
        sent = [(partial[0, s] + joined[s]).astype(jnp.bfloat16) for s in range(1, chips)]
        return partial[0, 0], joined[0], [chip_shift(sent[s - 1], s) for s in range(1, chips)]

    near, mate, received = section_stress(slip)
    stress_one = near + mate
    for part in received:
        stress_one = stress_one + part.astype(jnp.float32)
    velocity_one, drift_one = slip_rates(stress_one, state, load, friction_a)
    slip_mid = slip + STEP * velocity_one
    near, mate, received = section_stress(slip_mid)

    state_mid = state + STEP * drift_one
    softness = friction_a[:, None]
    scale = jnp.broadcast_to(1.0 / (2.0 * softness), slip.shape)
    shift = load * scale
    weight = 2.0 * jnp.exp(-state_mid / softness)
    slip_most = slip + 0.5 * STEP * velocity_one
    state_most = state + 0.5 * STEP * (drift_one + jnp.exp(-state_mid))
    return pl.pallas_call(
        finish_kernel,
        out_shape=(
            jax.ShapeDtypeStruct(slip.shape, jnp.float32),
            jax.ShapeDtypeStruct(slip.shape, jnp.float32),
        ),
        in_specs=[VMEM] * 8,
        out_specs=(pl.BlockSpec(memory_space=pl.ANY), pl.BlockSpec(memory_space=pl.ANY)),
        scratch_shapes=[
            pltpu.VMEM(slip.shape, jnp.float32),
            pltpu.VMEM(slip.shape, jnp.float32),
            pltpu.SemaphoreType.DMA((PARTS, 2)),
        ],
        compiler_params=PARAMS,
        cost_estimate=pl.CostEstimate(
            flops=16 * slip.size, bytes_accessed=32 * slip.size, transcendentals=2 * slip.size
        ),
    )(near, mate, jnp.stack(received), scale, shift, weight, slip_most, state_most)


def solution(mesh):
    placed = (
        P(("grp", "clu", "row"), None),
        P(("grp", "clu", "row"), None),
        P(("grp", "clu", "row"), None),
        P(("grp", "clu", "row")),
        P(("grp", "clu", "row"), None, None),
        P(("grp", "clu", "row"), None),
        P(("grp", "clu", "row"), None, None, None),
        P(("grp", "clu", "row"), None, None, None),
        P(("grp", "clu", "row"), None),
    )
    return jax.shard_map(
        body,
        mesh=mesh,
        in_specs=placed,
        out_specs=(P(("grp", "clu", "row"), None), P(("grp", "clu", "row"), None)),
        check_vma=False,
    )
```

```python
import functools

import jax
import jax.numpy as jnp
from jax import lax
from jax.experimental import pallas as pl
from jax.experimental.pallas import tpu as pltpu
from jax.sharding import PartitionSpec as P

REACH = 4
CORES = 2
STEP = 0.2
LOG_TWO = 0.6931471805599453
WIDTH = 4
PARTS = 4


def core_swap(array):
    devices = lax.axis_size("row")
    return lax.ppermute(array, "row", [(i, i ^ 1) for i in range(devices)])


def chip_shift(array, step):
    devices = lax.axis_size("row")
    pairs = [(i, (i + CORES * step) % devices) for i in range(devices)]
    return lax.ppermute(array, "row", pairs)


def group_shift(array, step):
    groups = lax.axis_size("clu")
    return lax.ppermute(array, "clu", [(i, (i + step) % groups) for i in range(groups)])


def end_shift(array, step):
    devices, groups = lax.axis_size("row"), lax.axis_size("clu")
    pairs = []
    for c in range(groups):
        for r in range(devices):
            to = c + step if r >= devices - CORES else c - step
            pairs.append((c * devices + r, to % groups * devices + r))
    return lax.ppermute(array, ("clu", "row"), pairs)


def around(value, size):
    value = jnp.where(value < 0, value + size, value)
    return jnp.where(value >= size, value - size, value)


def here():
    row = lax.axis_index("row")
    return lax.axis_index("clu"), lax.div(row, CORES), lax.rem(row, CORES)


def plan_kernel(leaf, own, pairs, plan, free, source_rows, target_rows):
    devices = lax.axis_size("row")
    chips, clusters = devices // CORES, devices * own
    group, chip, core = here()
    for near in range(-REACH, clusters + REACH):
        holder = near % clusters // own
        if near < 0:
            piece = chips + around(chip + 1, chips)
        elif near >= clusters:
            piece = chips + chip
        else:
            piece = around(chip - holder // CORES, chips)
        piece = ((core ^ (holder % CORES)) * 2 * chips + piece) * own + near % own
        source_rows[near + REACH] = piece * leaf
    for target in range(clusters):
        owner = target // own
        piece = (core ^ (owner % CORES)) * chips + around(owner // CORES - chip, chips)
        target_rows[target] = (piece * own + target % own) * leaf
        free[target] = 0
    for i in range(plan.shape[1]):
        plan[0, i] = 0
        plan[1, i] = 4 * chips * own * leaf
        plan[2, i] = 0

    def put(j, used):
        target = pairs[0, j] - group * clusters
        at = free[target]
        full = (at & (WIDTH - 1)) == 0
        at = jnp.where(full, used * WIDTH, at)
        free[target] = at + 1
        plan[0, at] = j
        plan[1, at] = source_rows[pairs[1, j] - group * clusters + REACH]
        plan[2, lax.shift_right_logical(at, WIDTH.bit_length() - 1)] = target_rows[target]
        return used + full.astype(jnp.int32)

    lax.fori_loop(0, pairs.shape[1], put, jnp.int32(0), unroll=8)


def stress_kernel(leaf, plan, blocks, window, far_u, far_v, *rest):
    targets, elems, ranks = far_u.shape
    groups, rank = far_v.shape[0], far_v.shape[1] // targets
    columns, out = rest[:groups], rest[groups]
    coeffs = [
        jnp.dot(far_v[s], columns[s][...], preferred_element_type=jnp.float32).astype(jnp.bfloat16)
        for s in range(groups)
    ]
    for t in range(targets):
        out[pl.ds(t * elems, elems), :] = jnp.dot(
            far_u[t],
            jnp.concatenate([c[t * rank : (t + 1) * rank] for c in coeffs], axis=0),
            preferred_element_type=jnp.float32,
        )
    products = []
    chunks = plan.shape[1] // WIDTH
    for i in range(chunks):
        places = range(i * WIDTH, (i + 1) * WIDTH)
        sources = [pl.ds(pl.multiple_of(plan[1, p], leaf), leaf) for p in places]
        products.append(
            jnp.dot(
                jnp.concatenate([blocks[plan[0, p]] for p in places], axis=1),
                jnp.concatenate([window[source, :] for source in sources], axis=0),
                preferred_element_type=jnp.float32,
            )
        )
    for i in range(chunks):
        out[pl.ds(pl.multiple_of(plan[2, i], leaf), leaf), :] += products[i]


def bases_kernel(ranks, far_u, far_v, by_target, by_source):
    targets, groups, rank, elems = far_u.shape
    chips = targets // CORES
    group, chip, core = here()
    toward = jnp.where(chip == chips - 1, -1, 1)
    steps = [(s + 1) // 2 if s % 2 else -(s // 2) for s in range(groups)]
    sources = [around(group + toward * step, groups) for step in steps]
    row = lax.broadcasted_iota(jnp.int32, (rank, elems), 0)
    for t in range(targets):
        other, ahead = t // chips, t % chips
        target = around(chip + ahead, chips) * CORES + (core ^ other)
        for s, source in enumerate(sources):
            kept = jnp.where(row < ranks[target, source], far_v[target, source].astype(jnp.float32), 0.0)
            by_source[s, t * rank : (t + 1) * rank, :] = kept.astype(jnp.bfloat16)
        bases = jnp.concatenate([far_u[target, source] for source in sources], axis=0)
        by_target[t] = bases.astype(jnp.float32).T.astype(jnp.bfloat16)


def finish_kernel(
    near, mate, received, scale, shift, weight, slip, state, slip_out, state_out, slips, states, done
):
    parts = done.shape[0]
    size = near.shape[0] // parts
    copies = []
    for part in range(parts):
        rows = pl.ds(part * size, size)
        stress = near[rows, :] + mate[rows, :]
        for s in range(received.shape[0]):
            stress = stress + received[s, rows, :].astype(jnp.float32)
        halved = stress * scale[rows, :] + shift[rows, :]
        velocity = weight[rows, :] * (jnp.exp(halved - LOG_TWO) - jnp.exp(-halved - LOG_TWO))
        speed = jnp.abs(velocity)
        slips[rows, :] = slip[rows, :] + 0.5 * STEP * velocity
        states[rows, :] = state[rows, :] - 0.5 * STEP * (speed / (1.0 + speed))
        for at, (held, out) in enumerate(((slips, slip_out), (states, state_out))):
            copies.append(pltpu.make_async_copy(held.at[rows], out.at[rows], done.at[part, at]))
            copies[-1].start()
    for copy in copies:
        copy.wait()


VMEM = pl.BlockSpec(memory_space=pltpu.VMEM)
SMEM = pl.BlockSpec(memory_space=pltpu.SMEM)
PARAMS = pltpu.CompilerParams(vmem_limit_bytes=16 * 1024 * 1024)


def planned_blocks(pairs, leaf, own):
    targets = lax.axis_size("row") * own
    chunks = (pairs.shape[1] + targets * (WIDTH - 1)) // WIDTH
    return pl.pallas_call(
        functools.partial(plan_kernel, leaf, own),
        out_shape=jax.ShapeDtypeStruct((3, chunks * WIDTH), jnp.int32),
        in_specs=[SMEM],
        out_specs=SMEM,
        scratch_shapes=[
            pltpu.SMEM((targets,), jnp.int32),
            pltpu.SMEM((targets + 2 * REACH,), jnp.int32),
            pltpu.SMEM((targets,), jnp.int32),
        ],
        compiler_params=PARAMS,
        cost_estimate=pl.CostEstimate(flops=4_000_000_000, bytes_accessed=10_000_000, transcendentals=0),
    )(pairs)


def arranged_bases(ranks, far_u, far_v):
    targets, groups, rank, elems = far_u.shape
    return pl.pallas_call(
        bases_kernel,
        out_shape=(
            jax.ShapeDtypeStruct((targets, elems, groups * rank), jnp.bfloat16),
            jax.ShapeDtypeStruct((groups, targets * rank, elems), jnp.bfloat16),
        ),
        in_specs=[SMEM, VMEM, VMEM],
        out_specs=(VMEM, VMEM),
        compiler_params=PARAMS,
        cost_estimate=pl.CostEstimate(flops=1024, bytes_accessed=1_000_000, transcendentals=0),
    )(ranks, far_u, far_v)


def partial_stress(plan, blocks, window, far_u, far_v, columns):
    targets, elems, ranks = far_u.shape
    count, leaf, _ = blocks.shape
    members, groups = window.shape[1], len(columns)
    return pl.pallas_call(
        functools.partial(stress_kernel, leaf),
        out_shape=jax.ShapeDtypeStruct((targets * elems, members), jnp.float32),
        in_specs=[SMEM] + [VMEM] * (4 + groups),
        out_specs=VMEM,
        compiler_params=PARAMS,
        cost_estimate=pl.CostEstimate(
            flops=2 * members * (count * leaf * leaf + 2 * targets * ranks * elems),
            bytes_accessed=2 * count * leaf * leaf + 4 * targets * elems * members,
            transcendentals=0,
        ),
    )(plan, blocks, window, far_u, far_v, *columns)


def slip_rates(stress, state, load, friction_a):
    softness = friction_a[:, None]
    halved = (stress + load) / (2.0 * softness)
    growth = jnp.exp(halved - LOG_TWO) - jnp.exp(-halved - LOG_TWO)
    velocity = 2.0 * jnp.exp(-state / softness) * growth
    speed = jnp.abs(velocity)
    drift = jnp.exp(-state) - speed / (1.0 + speed)
    return (velocity, drift)


def body(slip, state, load, friction_a, near_blocks, near_pairs, far_u, far_v, far_rank):
    elems, members = slip.shape
    leaf = near_blocks.shape[1]
    own = elems // leaf
    devices, groups = lax.axis_size("row"), lax.axis_size("clu")
    chips = devices // CORES
    assert REACH <= CORES * own
    spare = jnp.zeros((leaf, members), jnp.bfloat16)
    plans = []

    def planned(after):
        if not plans:
            pairs = near_pairs.T
            after, *tables = lax.optimization_barrier((after, far_rank, far_u, far_v))
            plans.append((planned_blocks(pairs, leaf, own), arranged_bases(*tables)))
        return after, plans[0]

    def section_stress(field):
        half = field.astype(jnp.bfloat16)
        near = jnp.concatenate([half] + [chip_shift(half, s) for s in range(1, chips)])
        straight = end_shift(half, 1)
        straight, (plan, bases) = planned(straight)
        column = [half, straight, end_shift(half, -1)]
        while len(column) < groups:
            column.append(end_shift(column[-2], 1 if len(column) % 2 else -1))
        ends = [chip_shift(straight, s) for s in range(1, chips)]
        ends, plan, bases = lax.optimization_barrier((ends, plan, bases))
        ends = jnp.concatenate([straight] + ends)
        others = [core_swap(near[:elems]), core_swap(near[elems:])]
        window = jnp.concatenate([near, ends] + others + [core_swap(ends), spare])
        partial = partial_stress(plan, near_blocks, window, *bases, column)
        partial = partial.reshape(CORES, chips, elems, members)
        joined = [core_swap(partial[1, s]) for s in range(chips)]
        sent = [(partial[0, s] + joined[s]).astype(jnp.bfloat16) for s in range(1, chips)]
        return partial[0, 0], joined[0], [chip_shift(sent[s - 1], s) for s in range(1, chips)]

    near, mate, received = section_stress(slip)
    stress_one = near + mate
    for part in received:
        stress_one = stress_one + part.astype(jnp.float32)
    velocity_one, drift_one = slip_rates(stress_one, state, load, friction_a)
    slip_mid = slip + STEP * velocity_one
    near, mate, received = section_stress(slip_mid)

    state_mid = state + STEP * drift_one
    softness = friction_a[:, None]
    scale = jnp.broadcast_to(1.0 / (2.0 * softness), slip.shape)
    shift = load * scale
    weight = 2.0 * jnp.exp(-state_mid / softness)
    slip_most = slip + 0.5 * STEP * velocity_one
    state_most = state + 0.5 * STEP * (drift_one + jnp.exp(-state_mid))
    return pl.pallas_call(
        finish_kernel,
        out_shape=(
            jax.ShapeDtypeStruct(slip.shape, jnp.float32),
            jax.ShapeDtypeStruct(slip.shape, jnp.float32),
        ),
        in_specs=[VMEM] * 8,
        out_specs=(pl.BlockSpec(memory_space=pl.ANY), pl.BlockSpec(memory_space=pl.ANY)),
        scratch_shapes=[
            pltpu.VMEM(slip.shape, jnp.float32),
            pltpu.VMEM(slip.shape, jnp.float32),
            pltpu.SemaphoreType.DMA((PARTS, 2)),
        ],
        compiler_params=PARAMS,
        cost_estimate=pl.CostEstimate(
            flops=16 * slip.size, bytes_accessed=32 * slip.size, transcendentals=2 * slip.size
        ),
    )(near, mate, jnp.stack(received), scale, shift, weight, slip_most, state_most)


def solution(mesh):
    placed = (
        P(("grp", "clu", "row"), None),
        P(("grp", "clu", "row"), None),
        P(("grp", "clu", "row"), None),
        P(("grp", "clu", "row")),
        P(("grp", "clu", "row"), None, None),
        P(("grp", "clu", "row"), None),
        P(("grp", "clu", "row"), None, None, None),
        P(("grp", "clu", "row"), None, None, None),
        P(("grp", "clu", "row"), None),
    )
    return jax.shard_map(
        body,
        mesh=mesh,
        in_specs=placed,
        out_specs=(P(("grp", "clu", "row"), None), P(("grp", "clu", "row"), None)),
        check_vma=False,
    )
```
